128 devices in a mesh: col: 8 (over y_hi, x), row: 16 (over y_lo, z, core).
Axes of the slice: x: 4, y: 4 (y_hi: 2, y_lo: 2; y = y_hi * 2 + y_lo), z: 4, core: 2. Of those that a mesh axis runs over, the one named last changes fastest.
Arguments:
- inputs: bfloat16 [16384, 4096], P(('col', 'row')), may hold values from -6 to 6
- leaf_maps: bfloat16 [16384, 4096], P(('col', 'row')), may hold values from -0.75 to 0.75
- expand_maps: bfloat16 [16384, 4096], P(('col', 'row')), may hold values from -0.75 to 0.75
- patterns: int32 [14, 16384], replicated, may hold values from 0 to 63
- translations: bfloat16 [64, 64, 128], replicated, may hold values from -0.5 to 0.5
Outputs:
- applied: bfloat16 [16384, 4096], P(('col', 'row'))
The draws below stay inside these ranges and needn't reach their ends.
All inputs are finite; a program needn't handle non-finite values.
Results may differ from the reference program's by a relative error of at most 0.029.
Values may be sent and summed in bfloat16 or wider, within the bound.
No kernel may reach another device: no remote copies, remote signals or barrier semaphores. Data moves between devices by JAX's collectives and lax.ppermute only.
A program may use at most 128 MiB of HBM per device.

```python
import jax
import jax.numpy as jnp
from jax import lax

LEAF = 64
RANK = 64
VECS = 64
DICT = 64
LOCAL_LEVELS = 7
COL_BITS = 3
ROW_BITS = 4
LEVELS = 14
BLOCKS = 16384


def place_ends(values, rng, smallest, largest):
    index_at = [jax.random.randint(jax.random.fold_in(rng, axis), (), 0, length) for axis, length in enumerate(values.shape)]
    widest = values.shape.index(max(values.shape))
    neighbour = index_at[:widest] + [(index_at[widest] + 1) % values.shape[widest]] + index_at[widest + 1:]
    return values.at[tuple(index_at)].set(smallest).at[tuple(neighbour)].set(largest)


def steps_of(stream_key, shape, shards, least, largest):
    loudness, own = 1.0, jax.random.fold_in(stream_key, 6)
    for dim, parts in shards:
        steps = jnp.exp(jax.random.uniform(jax.random.fold_in(own, dim), (parts,), jnp.float32, least / len(shards), largest / len(shards)))
        loudness = loudness * jnp.repeat(steps, shape[dim] // parts).reshape([-1 if axis == dim else 1 for axis in range(len(shape))])
    return loudness


def centred(rng, extent, spread, most, split=(), kind=jnp.bfloat16):
    array = jax.random.normal(rng, extent, jnp.float32) * spread
    if len(split) > 0:
        array = steps_of(rng, extent, split, -0.22, 0.18) * array
    return jnp.clip(array, min=-most, max=most).astype(kind)


def setup_inputs(seed: int = 0) -> dict:
    key_of = jax.random.split(jax.random.key(seed), 6)
    inputs = centred(key_of[0], (BLOCKS, LEAF * VECS), 1.0, 6.0, ((0, 128),))
    leaf_maps = centred(key_of[1], (BLOCKS, LEAF * RANK), LEAF ** -0.5, 0.75, ((0, 128),))
    expand_maps = centred(key_of[2], (BLOCKS, LEAF * RANK), RANK ** -0.5, 0.75, ((0, 128),))
    patterns = place_ends(jax.random.randint(key_of[3], (LEVELS, BLOCKS), 0, DICT), jax.random.fold_in(key_of[3], 1), 0, DICT - 1).astype(jnp.int32)
    translations = centred(key_of[4], (DICT, RANK, 2 * RANK), (2 * RANK) ** -0.5, 0.5)
    return dict(inputs=inputs, leaf_maps=leaf_maps, expand_maps=expand_maps, patterns=patterns, translations=translations)


def pair_flip(values, level_bit):
    count = values.shape[0]
    shaped = values.reshape((count >> (level_bit + 1), 2, 1 << level_bit) + values.shape[1:])
    return jnp.flip(shaped, 1).reshape(values.shape)


def grouped(function, arrays):
    group = min(BLOCKS, 4096)
    shaped = tuple(item.reshape((BLOCKS // group, group) + item.shape[1:]) for item in arrays)
    result = lax.map(lambda pieces: function(*pieces), shaped)
    return result.reshape((BLOCKS,) + result.shape[2:])


def reference(inputs, leaf_maps, expand_maps, patterns, translations):
    source = inputs.reshape(BLOCKS, LEAF, VECS)
    compress = leaf_maps.reshape(BLOCKS, LEAF, RANK)
    expand = expand_maps.reshape(BLOCKS, LEAF, RANK)

    def leaf_step(maps, values):
        return jnp.einsum("jlr,jlk->jrk", maps.astype(jnp.float32), values.astype(jnp.float32)).astype(jnp.bfloat16)

    state = grouped(leaf_step, (compress, source))

    def combine(own, partner, chosen):
        mats = translations[chosen].astype(jnp.float32)
        near = jnp.einsum("brt,btk->brk", mats[:, :, :RANK], own.astype(jnp.float32))
        far = jnp.einsum("brt,btk->brk", mats[:, :, RANK:], partner.astype(jnp.float32))
        return (near + far).astype(jnp.bfloat16)

    order_bits = [LOCAL_LEVELS + ROW_BITS + item for item in range(COL_BITS)]
    order_bits = order_bits + list(range(LOCAL_LEVELS))
    order_bits = order_bits + [LOCAL_LEVELS + item for item in range(ROW_BITS)]
    for level, level_bit in enumerate(order_bits):
        partner = pair_flip(state, level_bit)
        state = grouped(combine, (state, partner, patterns[level]))

    def final_step(maps, values):
        return jnp.einsum("jlr,jrk->jlk", maps.astype(jnp.float32), values.astype(jnp.float32)).astype(jnp.bfloat16)

    result = grouped(final_step, (expand, state))
    return result.reshape(BLOCKS, LEAF * VECS)
```

```python
import functools

import jax
import jax.numpy as jnp
from jax import lax
from jax.experimental import pallas as pl
from jax.experimental.pallas import tpu as pltpu
from jax.sharding import Mesh, PartitionSpec as P

LEAF = 64
RANK = 64
VECS = 64
WIDE = 2 * VECS
TILES = 64
AXES = ("yh", "x", "yl", "z", "core")
CHIPS = ("yh", "x", "yl", "z")


def left_half(shape):
    return lax.broadcasted_iota(jnp.int32, shape, len(shape) - 1) < VECS


def halves(tile):
    left = left_half(tile.shape)
    zero = jnp.zeros_like(tile)
    return jnp.where(left, tile, zero), jnp.where(left, zero, tile)


def swap_halves(tile):
    return jnp.concatenate([tile[:, VECS:], tile[:, :VECS]], axis=1)


def dot(lhs, rhs):
    return jnp.dot(lhs, rhs, preferred_element_type=jnp.float32).astype(jnp.bfloat16)


def tile_level(src, dst, near, swapped, chosen, bit, place=lambda tile: tile, unroll=4):
    def step(pair, carry):
        a = ((pair >> bit) << (bit + 1)) | (pair & ((1 << bit) - 1))
        b = a + (1 << bit)
        al, ar = halves(src[a])
        bl, br = halves(src[b])
        weights = jnp.concatenate([al, bl, ar, br], axis=0)
        for_a = jnp.concatenate([near[chosen(a, 0)], near[chosen(a, 1)]], axis=1)
        for_b = jnp.concatenate([swapped[chosen(b, 0)], swapped[chosen(b, 1)]], axis=1)
        out = dot(jnp.concatenate([for_a, for_b], axis=0), weights)
        dst[place(a)] = out[:RANK]
        dst[place(b)] = out[RANK:]
        return carry

    lax.fori_loop(0, TILES // 2, step, 0, unroll=unroll)


def lane_level(src, dst, near, chosen, unroll=4):
    def step(a, carry):
        tile = src[a]
        al, ar = halves(tile)
        bl, br = halves(swap_halves(tile))
        weights = jnp.concatenate([al, bl, ar, br], axis=0)
        for_a = jnp.concatenate([near[chosen(a, 0)], near[chosen(a, 1)]], axis=1)
        dst[a] = dot(for_a, weights)
        return carry

    lax.fori_loop(0, TILES, step, 0, unroll=unroll)


def other_level(src, partner, dst, near, chosen, unroll=4):
    def step(a, carry):
        al, ar = halves(src[a])
        bl, br = halves(partner[a])
        weights = jnp.concatenate([al, bl, ar, br], axis=0)
        for_a = jnp.concatenate([near[chosen(a, 0)], near[chosen(a, 1)]], axis=1)
        dst[a] = dot(for_a, weights)
        return carry

    lax.fori_loop(0, TILES, step, 0, unroll=unroll)


def leaf_kernel(maps, vectors, out):
    def step(group, carry):
        tile = group * 2
        box = (tile >> 3) * 16 + (tile & 7)
        order = (box, box + 8, box + 1, box + 9)
        v = jnp.concatenate([maps[j] for j in order], axis=0).T
        lhs = jnp.concatenate([v[:RANK], v[RANK:]], axis=1)
        zero = jnp.zeros((LEAF // 2, WIDE), jnp.bfloat16)
        even, odd = [], []
        for place, j in enumerate(order):
            raw = vectors[j]
            el, orr = halves(raw)
            turned = swap_halves(raw)
            ol, er = halves(turned)
            e, o = (el, ol) if place % 2 == 0 else (er, orr)
            even.append([e, zero] if place < 2 else [zero, e])
            odd.append([o, zero] if place < 2 else [zero, o])
        weights = jnp.concatenate([jnp.concatenate(r, axis=1) for r in even + odd], axis=0)
        both = dot(lhs, weights)
        out[tile] = both[:, :WIDE]
        out[tile + 1] = both[:, WIDE:]
        return carry

    lax.fori_loop(0, TILES // 2, step, 0, unroll=2)


def first_kernel(chosen_ref, state, near, swapped, out, one, two):
    def chosen(level):
        return lambda tile, half: chosen_ref[level * 128 + (tile >> 3) * 16 + half * 8 + (tile & 7)]

    bufs = [state, one, two, one, two, one, two]
    for level, bit in enumerate((3, 4, 5, 0, 1, 2)):
        tile_level(bufs[level], bufs[level + 1], near, swapped, chosen(level), bit)
    lane_level(two, out, near, chosen(6))


def second(chosen_ref, level):
    return lambda tile, half: chosen_ref[level * 128 + (tile & 7) * 16 + (tile >> 3) * 2 + half]


def second_kernel(chosen_ref, state, near, swapped, out, one, two):
    bufs = [state, one, two, out]
    for level, bit in enumerate((3, 4, 5)):
        tile_level(bufs[level], bufs[level + 1], near, swapped, second(chosen_ref, level), bit)


def third_kernel(chosen_ref, state, partner, near, swapped, out, one, two):
    other_level(state, partner, one, near, second(chosen_ref, 3))
    tile_level(one, two, near, swapped, second(chosen_ref, 4), 0)
    tile_level(two, one, near, swapped, second(chosen_ref, 5), 1)
    turn = lambda tile: (tile & 7) * 8 + (tile >> 3)
    tile_level(one, out, near, swapped, second(chosen_ref, 6), 2, place=turn)


def expand_kernel(state, maps, out):
    def step(tile, carry):
        box = (tile & 7) * 16 + (tile >> 3)
        both = state[tile]
        al, ar = halves(both)
        bl, br = halves(swap_halves(both))
        out[box] = dot(maps[box], jnp.concatenate([al, br], axis=0))
        out[box + 8] = dot(maps[box + 8], jnp.concatenate([bl, ar], axis=0))
        return carry

    lax.fori_loop(0, TILES, step, 0, unroll=4)


VM = pl.BlockSpec(memory_space=pltpu.VMEM)
SM = pl.BlockSpec(memory_space=pltpu.SMEM)
PARAMS = pltpu.CompilerParams(vmem_limit_bytes=32 * 1024 * 1024)
STATE = jax.ShapeDtypeStruct((TILES, RANK, WIDE), jnp.bfloat16)


def local(inputs, leaf_maps, expand_maps, patterns, translations):
    boxes = inputs.shape[0]
    col_place = lax.axis_index("yh") * 4 + lax.axis_index("x")
    row_low = lax.axis_index("yl") * 4 + lax.axis_index("z")
    core = lax.axis_index("core")
    scratch = [pltpu.VMEM(STATE.shape, STATE.dtype)] * 2

    swapped = jnp.concatenate([translations[:, :, RANK:], translations[:, :, :RANK]], axis=2)
    row = row_low * 2 + core
    first_chosen = lax.dynamic_slice(
        patterns[:7].reshape(7, 8, 2048), (0, 0, row * 128 + col_place * 16), (7, 8, 16)
    ).reshape(-1)
    second_chosen = lax.dynamic_slice(patterns, (7, col_place * 2048), (7, 2048))
    second_chosen = lax.dynamic_slice(
        second_chosen.reshape(7, 8, 2, 16, 8), (0, 0, core, 0, row_low), (7, 8, 1, 16, 1)
    ).reshape(-1)

    shaped = (boxes, LEAF // 2, WIDE)
    state = pl.pallas_call(
        leaf_kernel, out_shape=STATE, in_specs=[VM, VM], out_specs=VM, compiler_params=PARAMS
    )(leaf_maps.reshape(shaped), inputs.reshape(shaped))
    state = lax.all_to_all(state, ("yh", "x"), 0, 0, tiled=True)
    state = pl.pallas_call(
        first_kernel, out_shape=STATE, in_specs=[SM, VM, VM, VM], out_specs=VM,
        scratch_shapes=scratch, compiler_params=PARAMS,
    )(first_chosen, state, translations, swapped)
    state = lax.all_to_all(state, CHIPS, 0, 0, tiled=True)
    state = pl.pallas_call(
        second_kernel, out_shape=STATE, in_specs=[SM, VM, VM, VM], out_specs=VM,
        scratch_shapes=scratch, compiler_params=PARAMS,
    )(second_chosen, state, translations, swapped)
    partner = lax.ppermute(state, "core", [(0, 1), (1, 0)])
    state = pl.pallas_call(
        third_kernel, out_shape=STATE, in_specs=[SM, VM, VM, VM, VM], out_specs=VM,
        scratch_shapes=scratch, compiler_params=PARAMS,
    )(second_chosen, state, partner, translations, swapped)
    state = lax.all_to_all(state, ("yl", "z"), 0, 0, tiled=True)
    result = pl.pallas_call(
        expand_kernel, out_shape=jax.ShapeDtypeStruct(shaped, jnp.bfloat16),
        in_specs=[VM, VM], out_specs=VM, compiler_params=PARAMS,
    )(state, expand_maps.reshape(shaped))
    return result.reshape(boxes, LEAF * VECS)


def solution(mesh):
    fine = Mesh(mesh.devices.reshape(2, 4, 2, 4, 2), AXES)
    rows = P(AXES, None)
    return jax.shard_map(
        local, mesh=fine, in_specs=(rows, rows, rows, P(), P()), out_specs=rows, check_vma=False
    )
```

```python
import jax
import jax.numpy as jnp
from jax import lax
from jax.experimental import pallas as pl
from jax.experimental.pallas import tpu as pltpu
from jax.sharding import Mesh, PartitionSpec as P

LEAF = 64
RANK = 64
VECS = 64
WIDE = 2 * VECS
TILES = 64
AXES = ("yh", "x", "yl", "z", "core")
CHIPS = ("yh", "x", "yl", "z")


def left_half(shape):
    return lax.broadcasted_iota(jnp.int32, shape, len(shape) - 1) < VECS


def halves(tile):
    left = left_half(tile.shape)
    zero = jnp.zeros_like(tile)
    return jnp.where(left, tile, zero), jnp.where(left, zero, tile)


def swap_halves(tile):
    return jnp.concatenate([tile[:, VECS:], tile[:, :VECS]], axis=1)


def dot(lhs, rhs):
    return jnp.dot(lhs, rhs, preferred_element_type=jnp.float32).astype(jnp.bfloat16)


def tile_level(src, dst, near, swapped, chosen, bit, place=lambda tile: tile):
    for pair in range(TILES // 2):
        a = ((pair >> bit) << (bit + 1)) | (pair & ((1 << bit) - 1))
        b = a + (1 << bit)
        al, ar = halves(src[a])
        bl, br = halves(src[b])
        weights = jnp.concatenate([al, bl, ar, br], axis=0)
        for_a = jnp.concatenate([near[chosen(a, 0)], near[chosen(a, 1)]], axis=1)
        for_b = jnp.concatenate([swapped[chosen(b, 0)], swapped[chosen(b, 1)]], axis=1)
        out = dot(jnp.concatenate([for_a, for_b], axis=0), weights)
        dst[place(a)] = out[:RANK]
        dst[place(b)] = out[RANK:]


def lane_level(src, dst, near, chosen):
    for a in range(TILES):
        tile = src[a]
        al, ar = halves(tile)
        bl, br = halves(swap_halves(tile))
        weights = jnp.concatenate([al, bl, ar, br], axis=0)
        for_a = jnp.concatenate([near[chosen(a, 0)], near[chosen(a, 1)]], axis=1)
        dst[a] = dot(for_a, weights)


def other_level(src, partner, dst, near, chosen):
    for a in range(TILES):
        al, ar = halves(src[a])
        bl, br = halves(partner[a])
        weights = jnp.concatenate([al, bl, ar, br], axis=0)
        for_a = jnp.concatenate([near[chosen(a, 0)], near[chosen(a, 1)]], axis=1)
        dst[a] = dot(for_a, weights)


def leaf_kernel(maps, vectors, out):
    for group in range(TILES // 2):
        tile = group * 2
        box = (tile >> 3) * 16 + (tile & 7)
        order = (box, box + 8, box + 1, box + 9)
        v = jnp.concatenate([maps[j] for j in order], axis=0).T
        lhs = jnp.concatenate([v[:RANK], v[RANK:]], axis=1)
        zero = jnp.zeros((LEAF // 2, WIDE), jnp.bfloat16)
        even, odd = [], []
        for place, j in enumerate(order):
            raw = vectors[j]
            el, orr = halves(raw)
            turned = swap_halves(raw)
            ol, er = halves(turned)
            e, o = (el, ol) if place % 2 == 0 else (er, orr)
            even.append([e, zero] if place < 2 else [zero, e])
            odd.append([o, zero] if place < 2 else [zero, o])
        weights = jnp.concatenate([jnp.concatenate(r, axis=1) for r in even + odd], axis=0)
        both = dot(lhs, weights)
        out[tile] = both[:, :WIDE]
        out[tile + 1] = both[:, WIDE:]


def first_kernel(chosen_ref, state, near, swapped, out, one, two):
    def chosen(level):
        return lambda tile, half: chosen_ref[level * 128 + (tile >> 3) * 16 + half * 8 + (tile & 7)]

    bufs = [state, one, two, one, two, one, two]
    for level, bit in enumerate((3, 4, 5, 0, 1, 2)):
        tile_level(bufs[level], bufs[level + 1], near, swapped, chosen(level), bit)
    lane_level(two, out, near, chosen(6))


def second(chosen_ref, level):
    return lambda tile, half: chosen_ref[level * 128 + (tile & 7) * 16 + (tile >> 3) * 2 + half]


def second_kernel(chosen_ref, state, near, swapped, out, one, two):
    bufs = [state, one, two, out]
    for level, bit in enumerate((3, 4, 5)):
        tile_level(bufs[level], bufs[level + 1], near, swapped, second(chosen_ref, level), bit)


def third_kernel(chosen_ref, state, partner, near, swapped, out, one, two):
    other_level(state, partner, one, near, second(chosen_ref, 3))
    tile_level(one, two, near, swapped, second(chosen_ref, 4), 0)
    tile_level(two, one, near, swapped, second(chosen_ref, 5), 1)
    turn = lambda tile: (tile & 7) * 8 + (tile >> 3)
    tile_level(one, out, near, swapped, second(chosen_ref, 6), 2, place=turn)


def expand_kernel(state, maps, out):
    for tile in range(TILES):
        box = (tile & 7) * 16 + (tile >> 3)
        both = state[tile]
        al, ar = halves(both)
        bl, br = halves(swap_halves(both))
        out[box] = dot(maps[box], jnp.concatenate([al, br], axis=0))
        out[box + 8] = dot(maps[box + 8], jnp.concatenate([bl, ar], axis=0))


VM = pl.BlockSpec(memory_space=pltpu.VMEM)
SM = pl.BlockSpec(memory_space=pltpu.SMEM)
PARAMS = pltpu.CompilerParams(vmem_limit_bytes=32 * 1024 * 1024)
STATE = jax.ShapeDtypeStruct((TILES, RANK, WIDE), jnp.bfloat16)


def local(inputs, leaf_maps, expand_maps, patterns, translations):
    boxes = inputs.shape[0]
    col_place = lax.axis_index("yh") * 4 + lax.axis_index("x")
    row_low = lax.axis_index("yl") * 4 + lax.axis_index("z")
    core = lax.axis_index("core")
    scratch = [pltpu.VMEM(STATE.shape, STATE.dtype)] * 2

    swapped = jnp.concatenate([translations[:, :, RANK:], translations[:, :, :RANK]], axis=2)
    row = row_low * 2 + core
    first_chosen = lax.dynamic_slice(
        patterns[:7].reshape(7, 8, 2048), (0, 0, row * 128 + col_place * 16), (7, 8, 16)
    ).reshape(-1)
    second_chosen = lax.dynamic_slice(patterns, (7, col_place * 2048), (7, 2048))
    second_chosen = lax.dynamic_slice(
        second_chosen.reshape(7, 8, 2, 16, 8), (0, 0, core, 0, row_low), (7, 8, 1, 16, 1)
    ).reshape(-1)

    shaped = (boxes, LEAF // 2, WIDE)
    state = pl.pallas_call(
        leaf_kernel, out_shape=STATE, in_specs=[VM, VM], out_specs=VM, compiler_params=PARAMS
    )(leaf_maps.reshape(shaped), inputs.reshape(shaped))
    state = lax.all_to_all(state, ("yh", "x"), 0, 0, tiled=True)
    state = pl.pallas_call(
        first_kernel, out_shape=STATE, in_specs=[SM, VM, VM, VM], out_specs=VM,
        scratch_shapes=scratch, compiler_params=PARAMS,
    )(first_chosen, state, translations, swapped)
    state = lax.all_to_all(state, CHIPS, 0, 0, tiled=True)
    state = pl.pallas_call(
        second_kernel, out_shape=STATE, in_specs=[SM, VM, VM, VM], out_specs=VM,
        scratch_shapes=scratch, compiler_params=PARAMS,
    )(second_chosen, state, translations, swapped)
    partner = lax.ppermute(state, "core", [(0, 1), (1, 0)])
    state = pl.pallas_call(
        third_kernel, out_shape=STATE, in_specs=[SM, VM, VM, VM, VM], out_specs=VM,
        scratch_shapes=scratch, compiler_params=PARAMS,
    )(second_chosen, state, partner, translations, swapped)
    state = lax.all_to_all(state, ("yl", "z"), 0, 0, tiled=True)
    result = pl.pallas_call(
        expand_kernel, out_shape=jax.ShapeDtypeStruct(shaped, jnp.bfloat16),
        in_specs=[VM, VM], out_specs=VM, compiler_params=PARAMS,
    )(state, expand_maps.reshape(shaped))
    return result.reshape(boxes, LEAF * VECS)


def solution(mesh):
    fine = Mesh(mesh.devices.reshape(2, 4, 2, 4, 2), AXES)
    rows = P(AXES, None)
    return jax.shard_map(
        local, mesh=fine, in_specs=(rows, rows, rows, P(), P()), out_specs=rows, check_vma=False
    )
```

```python
import functools

import jax
import jax.numpy as jnp
from jax import lax
from jax.experimental import pallas as pl
from jax.experimental.pallas import tpu as pltpu
from jax.sharding import Mesh, PartitionSpec as P

LEAF = 64
RANK = 64
VECS = 64
WIDE = 2 * VECS
TILES = 64
AXES = ("yh", "x", "yl", "z", "core")
CHIPS = ("yh", "x", "yl", "z")


def left_half(shape):
    return lax.broadcasted_iota(jnp.int32, shape, len(shape) - 1) < VECS


def halves(tile):
    left = left_half(tile.shape)
    zero = jnp.zeros_like(tile)
    return jnp.where(left, tile, zero), jnp.where(left, zero, tile)


def swap_halves(tile):
    return jnp.concatenate([tile[:, VECS:], tile[:, :VECS]], axis=1)


def dot(lhs, rhs):
    return jnp.dot(lhs, rhs, preferred_element_type=jnp.float32).astype(jnp.bfloat16)


def tile_level(load, store, near, swapped, chosen, bit, tiles):
    for a in tiles:
        if a >> bit & 1:
            continue
        b = a + (1 << bit)
        al, ar = halves(load(a))
        bl, br = halves(load(b))
        weights = jnp.concatenate([al, bl, ar, br], axis=0)
        for_a = jnp.concatenate([near[chosen(a, 0)], near[chosen(a, 1)]], axis=1)
        for_b = jnp.concatenate([swapped[chosen(b, 0)], swapped[chosen(b, 1)]], axis=1)
        out = dot(jnp.concatenate([for_a, for_b], axis=0), weights)
        store(a, out[:RANK])
        store(b, out[RANK:])


def lane_level(load, store, near, chosen, tiles):
    for a in tiles:
        tile = load(a)
        al, ar = halves(tile)
        bl, br = halves(swap_halves(tile))
        weights = jnp.concatenate([al, bl, ar, br], axis=0)
        store(a, dot(jnp.concatenate([near[chosen(a, 0)], near[chosen(a, 1)]], axis=1), weights))


def other_level(load, load_partner, store, near, chosen, tiles):
    for a in tiles:
        al, ar = halves(load(a))
        bl, br = halves(load_partner(a))
        weights = jnp.concatenate([al, bl, ar, br], axis=0)
        store(a, dot(jnp.concatenate([near[chosen(a, 0)], near[chosen(a, 1)]], axis=1), weights))


def getter(ref):
    return lambda tile: ref[tile]


def setter(ref):
    def store(tile, value):
        ref[tile] = value

    return store


def col_place():
    return lax.axis_index("yh") * 4 + lax.axis_index("x")


def row_low():
    return lax.axis_index("yl") * 4 + lax.axis_index("z")


def leaf_kernel(maps, vectors, out, v_in, x_in, made, v_sem, x_sem, out_sem):
    copies = []
    for n in range(2):
        rows = pl.ds(n * 64, 64)
        copies.append(
            (
                pltpu.make_async_copy(maps.at[rows], v_in.at[rows], v_sem.at[n]),
                pltpu.make_async_copy(vectors.at[rows], x_in.at[rows], x_sem.at[n]),
            )
        )
        for copy in copies[-1]:
            copy.start()
    zero = jnp.zeros((LEAF // 2, WIDE), jnp.bfloat16)
    sent = []
    for h in range(8):
        if h % 4 == 0:
            for copy in copies[h // 4]:
                copy.wait()
        rows = pl.ds(h * 16, 16)
        maps_here = v_in[rows].reshape(16, LEAF // 2, WIDE)
        vectors_here = x_in[rows].reshape(16, LEAF // 2, WIDE)
        for tile in range(0, 8, 2):
            order = [tile + step for step in (0, 8, 1, 9)]
            v = jnp.concatenate([maps_here[j] for j in order], axis=0).T
            lhs = jnp.concatenate([v[:RANK], v[RANK:]], axis=1)
            even, odd = [], []
            for place, j in enumerate(order):
                raw = vectors_here[j]
                el, orr = halves(raw)
                ol, er = halves(swap_halves(raw))
                e, o = (el, ol) if place % 2 == 0 else (er, orr)
                even.append([e, zero] if place < 2 else [zero, e])
                odd.append([o, zero] if place < 2 else [zero, o])
            weights = jnp.concatenate([jnp.concatenate(r, axis=1) for r in even + odd], axis=0)
            both = dot(lhs, weights)
            made[h * 8 + tile] = both[:, :WIDE]
            made[h * 8 + tile + 1] = both[:, WIDE:]
        if h % 4 == 3:
            done = pl.ds((h - 3) * 8, 32)
            sent.append(pltpu.make_async_copy(made.at[done], out.at[done], out_sem.at[h // 4]))
            sent[-1].start()
    for copy in sent:
        copy.wait()


def table_kernel(
    patterns, late_patterns, translations, first_chosen, second_chosen, near, swapped, p_in, p_sem, t_sem
):
    table = pltpu.make_async_copy(translations, near, t_sem)
    table.start()
    core = lax.axis_index("core")
    lookups = []
    for k in range(8):
        columns = pl.ds(pl.multiple_of((k * 16 + row_low() * 2 + core) * 128, 128), 128)
        lookups.append(pltpu.make_async_copy(patterns.at[pl.ds(0, 8), columns], p_in.at[k], p_sem.at[k]))
        lookups[k].start()
    lane = lax.broadcasted_iota(jnp.int32, (8, 128), 1)
    first = second = jnp.zeros((8, 128), jnp.int32)
    for k in range(8):
        turn = jnp.remainder(k - row_low() + 128, 128)
        rows = late_patterns[:, pl.ds(pl.multiple_of((k * 2 + core) * 128, 128), 128)]
        second = jnp.where((lane & 7) == k, pltpu.roll(rows, turn, 1), second)
    second_chosen[...] = second
    for k in range(8):
        lookups[k].wait()
    for k in range(8):
        turn = jnp.remainder((k - col_place()) * 16 + 128, 128)
        first = jnp.where((lane >> 4) == k, pltpu.roll(p_in[k], turn, 1), first)
    first_chosen[...] = first
    table.wait()
    for m in range(near.shape[0]):
        swapped[m] = swap_halves(near[m])


def lookup(chosen_ref, level):
    return lambda tile, half: chosen_ref[level, (tile >> 3) * 16 + half * 8 + (tile & 7)]


def first_kernel(chosen_ref, state, near, swapped, out, one, two):
    every = range(TILES)
    bufs = [state, one, two, one, two, one, two]
    for level, bit in enumerate((3, 4, 5, 0, 1, 2)):
        tile_level(
            getter(bufs[level]), setter(bufs[level + 1]), near, swapped, lookup(chosen_ref, level), bit, every
        )
    lane_level(getter(two), setter(out), near, lookup(chosen_ref, 6), every)


HALVES = [[tile for tile in range(TILES) if tile >> 2 & 1 == n] for n in range(2)]


def packed(tile):
    return (tile >> 3) * 4 + (tile & 3)


def second_kernel(part, chosen_ref, state, near, swapped, out, one, two):
    tiles = HALVES[part]

    def store_out(tile, value):
        out[packed(tile)] = value

    loads = [getter(state), getter(one), getter(two)]
    stores = [setter(one), setter(two), store_out]
    for level in range(3):
        tile_level(
            loads[level], stores[level], near, swapped, lookup(chosen_ref, 1 + level), 3 + level, tiles
        )


def row_levels(part, chosen_ref, state, partner, near, swapped, one, two, store):
    tiles = HALVES[part]
    load, load_partner = (lambda tile, ref=ref: ref[packed(tile)] for ref in (state, partner))
    other_level(load, load_partner, setter(one), near, lookup(chosen_ref, 4), tiles)
    tile_level(getter(one), setter(two), near, swapped, lookup(chosen_ref, 5), 0, tiles)
    tile_level(getter(two), store, near, swapped, lookup(chosen_ref, 6), 1, tiles)


def third_kernel(chosen_ref, state, partner, near, swapped, out, one, two):
    def store(tile, value):
        out[packed(tile)] = value

    row_levels(0, chosen_ref, state, partner, near, swapped, one, two, store)


def fourth_kernel(chosen_ref, earlier, state, partner, near, swapped, out, one, two):
    row_levels(1, chosen_ref, state, partner, near, swapped, one, two, setter(one))
    load = lambda tile: one[tile] if tile >> 2 & 1 else earlier[packed(tile)]

    def store(tile, value):
        out[(tile & 7) * 8 + (tile >> 3)] = value

    tile_level(load, store, near, swapped, lookup(chosen_ref, 7), 2, range(TILES))


def expand_kernel(state, maps, out, made, sem):
    copies = []
    zero = jnp.zeros((LEAF // 2, WIDE), jnp.bfloat16)
    for h in range(8):
        rows = pl.ds(h * 16, 16)
        maps_here = maps[rows].reshape(16, LEAF // 2, WIDE)
        results = [None] * 16
        for q in range(8):
            both = state[q * 8 + h]
            al, ar = halves(both)
            bl, br = halves(swap_halves(both))
            lhs = [[maps_here[q], zero], [zero, maps_here[q + 8]]]
            lhs = jnp.concatenate([jnp.concatenate(r, axis=1) for r in lhs], axis=0)
            two = dot(lhs, jnp.concatenate([al, br, bl, ar], axis=0))
            results[q], results[q + 8] = two[: LEAF // 2], two[LEAF // 2 :]
        made[rows] = jnp.stack(results, axis=0).reshape(16, LEAF * VECS)
        copies.append(pltpu.make_async_copy(made.at[rows], out.at[rows], sem.at[h]))
        copies[-1].start()
    for copy in copies:
        copy.wait()


VM = pl.BlockSpec(memory_space=pltpu.VMEM)
SM = pl.BlockSpec(memory_space=pltpu.SMEM)
HB = pl.BlockSpec(memory_space=pltpu.HBM)
PARAMS = pltpu.CompilerParams(vmem_limit_bytes=32 * 1024 * 1024)
STATE = jax.ShapeDtypeStruct((TILES, RANK, WIDE), jnp.bfloat16)
HALF = jax.ShapeDtypeStruct((TILES // 2, RANK, WIDE), jnp.bfloat16)


def make_tables(patterns, translations):
    late_patterns = lax.dynamic_slice(patterns, (6, col_place() * 2048), (8, 2048))
    table = jax.ShapeDtypeStruct(translations.shape, translations.dtype)
    return pl.pallas_call(
        table_kernel,
        out_shape=[
            jax.ShapeDtypeStruct((8, 128), jnp.int32), jax.ShapeDtypeStruct((8, 128), jnp.int32), table, table,
        ],
        in_specs=[HB, VM, HB], out_specs=[VM] * 4,
        scratch_shapes=[
            pltpu.VMEM((8, 8, 128), jnp.int32), pltpu.SemaphoreType.DMA((8,)), pltpu.SemaphoreType.DMA,
        ],
        compiler_params=PARAMS,
    )(patterns, late_patterns, translations)


def local(inputs, leaf_maps, expand_maps, patterns, translations):
    rows = jax.ShapeDtypeStruct(inputs.shape, jnp.bfloat16)
    scratch = [pltpu.VMEM(STATE.shape, STATE.dtype)] * 2
    state = pl.pallas_call(
        leaf_kernel, out_shape=STATE, in_specs=[HB] * 2, out_specs=HB,
        scratch_shapes=[pltpu.VMEM(rows.shape, rows.dtype)] * 2
        + [pltpu.VMEM(STATE.shape, STATE.dtype)] + [pltpu.SemaphoreType.DMA((2,))] * 3,
        compiler_params=pltpu.CompilerParams(vmem_limit_bytes=63 * 1024 * 1024),
    )(leaf_maps, inputs)
    first_chosen, second_chosen, near, swapped = make_tables(patterns, translations)
    state = lax.all_to_all(state, ("yh", "x"), 0, 0, tiled=True)
    state = pl.pallas_call(
        first_kernel, out_shape=STATE, in_specs=[SM, VM, VM, VM], out_specs=VM,
        scratch_shapes=scratch, compiler_params=PARAMS,
    )(first_chosen, state, near, swapped)
    state = lax.all_to_all(state, CHIPS, 0, 0, tiled=True)
    parts, partners = [], []
    for n in range(2):
        parts.append(
            pl.pallas_call(
                functools.partial(second_kernel, n), out_shape=HALF, in_specs=[SM, VM, VM, VM], out_specs=VM,
                scratch_shapes=scratch, compiler_params=PARAMS,
            )(second_chosen, state, near, swapped)
        )
        partners.append(lax.ppermute(parts[n], "core", [(0, 1), (1, 0)]))
    earlier = pl.pallas_call(
        third_kernel, out_shape=HALF, in_specs=[SM, VM, VM, VM, VM], out_specs=VM,
        scratch_shapes=scratch, compiler_params=PARAMS,
    )(second_chosen, parts[0], partners[0], near, swapped)
    state = pl.pallas_call(
        fourth_kernel, out_shape=STATE, in_specs=[SM, VM, VM, VM, VM, VM], out_specs=VM,
        scratch_shapes=scratch, compiler_params=PARAMS,
    )(second_chosen, earlier, parts[1], partners[1], near, swapped)
    state = lax.all_to_all(state, ("yl", "z"), 0, 0, tiled=True)
    return pl.pallas_call(
        expand_kernel, out_shape=rows, in_specs=[VM, VM], out_specs=HB,
        scratch_shapes=[pltpu.VMEM(rows.shape, rows.dtype), pltpu.SemaphoreType.DMA((8,))],
        compiler_params=PARAMS,
    )(state, expand_maps)


def solution(mesh):
    fine = Mesh(mesh.devices.reshape(2, 4, 2, 4, 2), AXES)
    rows = P(AXES, None)
    return jax.shard_map(
        local, mesh=fine, in_specs=(rows, rows, rows, P(), P()), out_specs=rows, check_vma=False
    )
```

```python
import functools

import jax
import jax.numpy as jnp
from jax import lax
from jax.experimental import pallas as pl
from jax.experimental.pallas import tpu as pltpu
from jax.sharding import Mesh, PartitionSpec as P

LEAF = 64
RANK = 64
VECS = 64
WIDE = 2 * VECS
TILES = 64
AXES = ("yh", "x", "yl", "z", "core")
CHIPS = ("z", "x", "yh", "yl")


def left_half(shape):
    return lax.broadcasted_iota(jnp.int32, shape, len(shape) - 1) < VECS


def halves(tile):
    left = left_half(tile.shape)
    zero = jnp.zeros_like(tile)
    return jnp.where(left, tile, zero), jnp.where(left, zero, tile)


def swap_halves(tile):
    return jnp.concatenate([tile[:, VECS:], tile[:, :VECS]], axis=1)


def dot(lhs, rhs):
    return jnp.dot(lhs, rhs, preferred_element_type=jnp.float32).astype(jnp.bfloat16)


def tile_level(load, store, near, swapped, chosen, bit, tiles):
    for a in tiles:
        if a >> bit & 1:
            continue
        b = a + (1 << bit)
        al, ar = halves(load(a))
        bl, br = halves(load(b))
        weights = jnp.concatenate([al, bl, ar, br], axis=0)
        for_a = jnp.concatenate([near[chosen(a, 0)], near[chosen(a, 1)]], axis=1)
        for_b = jnp.concatenate([swapped[chosen(b, 0)], swapped[chosen(b, 1)]], axis=1)
        out = dot(jnp.concatenate([for_a, for_b], axis=0), weights)
        store(a, out[:RANK])
        store(b, out[RANK:])


def lane_level(load, store, near, chosen, tiles):
    for a in tiles:
        tile = load(a)
        al, ar = halves(tile)
        bl, br = halves(swap_halves(tile))
        weights = jnp.concatenate([al, bl, ar, br], axis=0)
        store(a, dot(jnp.concatenate([near[chosen(a, 0)], near[chosen(a, 1)]], axis=1), weights))


def other_level(load, load_partner, store, near, chosen, tiles):
    for a in tiles:
        al, ar = halves(load(a))
        bl, br = halves(load_partner(a))
        weights = jnp.concatenate([al, bl, ar, br], axis=0)
        store(a, dot(jnp.concatenate([near[chosen(a, 0)], near[chosen(a, 1)]], axis=1), weights))


def getter(ref):
    return lambda tile: ref[tile]


def setter(ref):
    def store(tile, value):
        ref[tile] = value

    return store


def col_place():
    return lax.axis_index("yh") * 4 + lax.axis_index("x")


def row_low():
    return lax.axis_index("yl") * 4 + lax.axis_index("z")


def leaf_kernel(maps, vectors, out, v_in, x_in, made, v_sem, x_sem, out_sem):
    copies = []
    for n in range(2):
        rows = pl.ds(n * 64, 64)
        copies.append(
            (
                pltpu.make_async_copy(maps.at[rows], v_in.at[rows], v_sem.at[n]),
                pltpu.make_async_copy(vectors.at[rows], x_in.at[rows], x_sem.at[n]),
            )
        )
        for copy in copies[-1]:
            copy.start()
    zero = jnp.zeros((LEAF // 2, WIDE), jnp.bfloat16)
    sent = []
    for h in range(8):
        if h % 4 == 0:
            for copy in copies[h // 4]:
                copy.wait()
        rows = pl.ds(h * 16, 16)
        maps_here = v_in[rows].reshape(16, LEAF // 2, WIDE)
        vectors_here = x_in[rows].reshape(16, LEAF // 2, WIDE)
        for tile in range(0, 8, 2):
            order = [tile + step for step in (0, 8, 1, 9)]
            v = jnp.concatenate([maps_here[j] for j in order], axis=0).T
            lhs = jnp.concatenate([v[:RANK], v[RANK:]], axis=1)
            even, odd = [], []
            for place, j in enumerate(order):
                raw = vectors_here[j]
                el, orr = halves(raw)
                ol, er = halves(swap_halves(raw))
                e, o = (el, ol) if place % 2 == 0 else (er, orr)
                even.append([e, zero] if place < 2 else [zero, e])
                odd.append([o, zero] if place < 2 else [zero, o])
            weights = jnp.concatenate([jnp.concatenate(r, axis=1) for r in even + odd], axis=0)
            both = dot(lhs, weights)
            made[h * 8 + tile] = both[:, :WIDE]
            made[h * 8 + tile + 1] = both[:, WIDE:]
        if h % 4 == 3:
            done = pl.ds((h - 3) * 8, 32)
            sent.append(pltpu.make_async_copy(made.at[done], out.at[done], out_sem.at[h // 4]))
            sent[-1].start()
    for copy in sent:
        copy.wait()


def table_kernel(
    patterns, late_patterns, translations, first_chosen, second_chosen, near, swapped, p_in, p_sem, t_sem
):
    table = pltpu.make_async_copy(translations, near, t_sem)
    table.start()
    core = lax.axis_index("core")
    lookups = []
    for k in range(8):
        columns = pl.ds(pl.multiple_of((k * 16 + row_low() * 2 + core) * 128, 128), 128)
        lookups.append(pltpu.make_async_copy(patterns.at[pl.ds(0, 8), columns], p_in.at[k], p_sem.at[k]))
        lookups[k].start()
    lane = lax.broadcasted_iota(jnp.int32, (8, 128), 1)
    first = second = jnp.zeros((8, 128), jnp.int32)
    for k in range(8):
        turn = jnp.remainder(k - row_low() + 128, 128)
        rows = late_patterns[:, pl.ds(pl.multiple_of((k * 2 + core) * 128, 128), 128)]
        second = jnp.where((lane & 7) == k, pltpu.roll(rows, turn, 1), second)
    second_chosen[...] = second
    for k in range(8):
        lookups[k].wait()
    for k in range(8):
        turn = jnp.remainder((k - col_place()) * 16 + 128, 128)
        first = jnp.where((lane >> 4) == k, pltpu.roll(p_in[k], turn, 1), first)
    first_chosen[...] = first
    table.wait()
    for m in range(near.shape[0]):
        swapped[m] = swap_halves(near[m])


def chip_order(tile):
    col, row = tile >> 3, tile & 7
    return (row & 3) * 16 + (col & 3) * 4 + (col >> 2) * 2 + (row >> 2)


def lane_of(tile, half):
    return (tile >> 3) * 16 + half * 8 + (tile & 7)


def lookup(chosen_ref, level):
    row = chosen_ref[level : level + 1, :]
    return lambda tile, half: row[0, lane_of(tile, half)]


def first_kernel(chosen_ref, state, near, swapped, out, one, two):
    every = range(TILES)
    bufs = [state, one, two, one, two, one, two]
    for level, bit in enumerate((3, 4, 5, 0, 1, 2)):
        tile_level(
            getter(bufs[level]), setter(bufs[level + 1]), near, swapped, lookup(chosen_ref, level), bit, every
        )

    def store(tile, value):
        out[chip_order(tile)] = value

    lane_level(getter(two), store, near, lookup(chosen_ref, 6), every)


HALVES = [[tile for tile in range(TILES) if tile >> 2 & 1 == n] for n in range(2)]


def packed(tile):
    return (tile >> 3) * 4 + (tile & 3)


def second_kernel(part, chosen_ref, state, near, swapped, out, one, two):
    tiles = HALVES[part]

    def store_out(tile, value):
        out[packed(tile)] = value

    loads = [lambda tile: state[chip_order(tile)], getter(one), getter(two)]
    stores = [setter(one), setter(two), store_out]
    for level in range(3):
        tile_level(
            loads[level], stores[level], near, swapped, lookup(chosen_ref, 1 + level), 3 + level, tiles
        )


def row_levels(part, chosen_ref, state, partner, near, swapped, one, two, store):
    tiles = HALVES[part]
    load, load_partner = (lambda tile, ref=ref: ref[packed(tile)] for ref in (state, partner))
    other_level(load, load_partner, setter(one), near, lookup(chosen_ref, 4), tiles)
    tile_level(getter(one), setter(two), near, swapped, lookup(chosen_ref, 5), 0, tiles)
    tile_level(getter(two), store, near, swapped, lookup(chosen_ref, 6), 1, tiles)


def third_kernel(chosen_ref, state, partner, near, swapped, out, one, two):
    def store(tile, value):
        out[packed(tile)] = value

    row_levels(0, chosen_ref, state, partner, near, swapped, one, two, store)


def fourth_kernel(chosen_ref, earlier, state, partner, near, swapped, out, one, two):
    row_levels(1, chosen_ref, state, partner, near, swapped, one, two, setter(one))
    load = lambda tile: one[tile] if tile >> 2 & 1 else earlier[packed(tile)]

    def store(tile, value):
        out[(tile & 7) * 8 + (tile >> 3)] = value

    tile_level(load, store, near, swapped, lookup(chosen_ref, 7), 2, range(TILES))


def expand_kernel(state, maps, out, made, sem):
    copies = []
    zero = jnp.zeros((LEAF // 2, WIDE), jnp.bfloat16)
    for h in range(8):
        rows = pl.ds(h * 16, 16)
        maps_here = maps[rows].reshape(16, LEAF // 2, WIDE)
        results = [None] * 16
        for q in range(8):
            both = state[q * 8 + h]
            al, ar = halves(both)
            bl, br = halves(swap_halves(both))
            lhs = [[maps_here[q], zero], [zero, maps_here[q + 8]]]
            lhs = jnp.concatenate([jnp.concatenate(r, axis=1) for r in lhs], axis=0)
            two = dot(lhs, jnp.concatenate([al, br, bl, ar], axis=0))
            results[q], results[q + 8] = two[: LEAF // 2], two[LEAF // 2 :]
        made[rows] = jnp.stack(results, axis=0).reshape(16, LEAF * VECS)
        copies.append(pltpu.make_async_copy(made.at[rows], out.at[rows], sem.at[h]))
        copies[-1].start()
    for copy in copies:
        copy.wait()


VM = pl.BlockSpec(memory_space=pltpu.VMEM)
HB = pl.BlockSpec(memory_space=pltpu.HBM)
PARAMS = pltpu.CompilerParams(vmem_limit_bytes=32 * 1024 * 1024)
STATE = jax.ShapeDtypeStruct((TILES, RANK, WIDE), jnp.bfloat16)
HALF = jax.ShapeDtypeStruct((TILES // 2, RANK, WIDE), jnp.bfloat16)


def make_tables(patterns, translations):
    late_patterns = lax.dynamic_slice(patterns, (6, col_place() * 2048), (8, 2048))
    table = jax.ShapeDtypeStruct(translations.shape, translations.dtype)
    return pl.pallas_call(
        table_kernel,
        out_shape=[
            jax.ShapeDtypeStruct((8, 128), jnp.int32), jax.ShapeDtypeStruct((8, 128), jnp.int32), table, table,
        ],
        in_specs=[HB, VM, HB], out_specs=[VM] * 4,
        scratch_shapes=[
            pltpu.VMEM((8, 8, 128), jnp.int32), pltpu.SemaphoreType.DMA((8,)), pltpu.SemaphoreType.DMA,
        ],
        compiler_params=PARAMS,
    )(patterns, late_patterns, translations)


def local(inputs, leaf_maps, expand_maps, patterns, translations):
    rows = jax.ShapeDtypeStruct(inputs.shape, jnp.bfloat16)
    scratch = [pltpu.VMEM(STATE.shape, STATE.dtype)] * 2
    state = pl.pallas_call(
        leaf_kernel, out_shape=STATE, in_specs=[HB] * 2, out_specs=HB,
        scratch_shapes=[pltpu.VMEM(rows.shape, rows.dtype)] * 2
        + [pltpu.VMEM(STATE.shape, STATE.dtype)] + [pltpu.SemaphoreType.DMA((2,))] * 3,
        compiler_params=pltpu.CompilerParams(vmem_limit_bytes=63 * 1024 * 1024),
    )(leaf_maps, inputs)
    first_chosen, second_chosen, near, swapped = make_tables(patterns, translations)
    state = lax.all_to_all(state, ("yh", "x"), 0, 0, tiled=True)
    state = pl.pallas_call(
        first_kernel, out_shape=STATE, in_specs=[VM, VM, VM, VM], out_specs=VM,
        scratch_shapes=scratch, compiler_params=PARAMS,
    )(first_chosen, state, near, swapped)
    state = lax.all_to_all(state, CHIPS, 0, 0, tiled=True)
    parts, partners = [], []
    for n in range(2):
        parts.append(
            pl.pallas_call(
                functools.partial(second_kernel, n), out_shape=HALF, in_specs=[VM, VM, VM, VM], out_specs=VM,
                scratch_shapes=scratch, compiler_params=PARAMS,
            )(second_chosen, state, near, swapped)
        )
        partners.append(lax.ppermute(parts[n], "core", [(0, 1), (1, 0)]))
    earlier = pl.pallas_call(
        third_kernel, out_shape=HALF, in_specs=[VM, VM, VM, VM, VM], out_specs=VM,
        scratch_shapes=scratch, compiler_params=PARAMS,
    )(second_chosen, parts[0], partners[0], near, swapped)
    state = pl.pallas_call(
        fourth_kernel, out_shape=STATE, in_specs=[VM, VM, VM, VM, VM, VM], out_specs=VM,
        scratch_shapes=scratch, compiler_params=PARAMS,
    )(second_chosen, earlier, parts[1], partners[1], near, swapped)
    state = lax.all_to_all(state, ("yl", "z"), 0, 0, tiled=True)
    return pl.pallas_call(
        expand_kernel, out_shape=rows, in_specs=[VM, VM], out_specs=HB,
        scratch_shapes=[pltpu.VMEM(rows.shape, rows.dtype), pltpu.SemaphoreType.DMA((8,))],
        compiler_params=PARAMS,
    )(state, expand_maps)


def solution(mesh):
    fine = Mesh(mesh.devices.reshape(2, 4, 2, 4, 2), AXES)
    rows = P(AXES, None)
    return jax.shard_map(
        local, mesh=fine, in_specs=(rows, rows, rows, P(), P()), out_specs=rows, check_vma=False
    )
```

```python
import functools

import jax
import jax.numpy as jnp
from jax import lax
from jax.experimental import pallas as pl
from jax.experimental.pallas import tpu as pltpu
from jax.sharding import Mesh, PartitionSpec as P

LEAF = 64
RANK = 64
VECS = 64
WIDE = 2 * VECS
TILES = 64
AXES = ("yh", "x", "yl", "z", "core")
CHIPS = ("x", "z", "yh", "yl")


def left_half(shape):
    return lax.broadcasted_iota(jnp.int32, shape, len(shape) - 1) < VECS


def halves(tile):
    left = left_half(tile.shape)
    zero = jnp.zeros_like(tile)
    return jnp.where(left, tile, zero), jnp.where(left, zero, tile)


def swap_halves(tile):
    return jnp.concatenate([tile[:, VECS:], tile[:, :VECS]], axis=1)


def dot(lhs, rhs):
    return jnp.dot(lhs, rhs, preferred_element_type=jnp.float32).astype(jnp.bfloat16)


def tile_level(load, store, near, swapped, chosen, bit, tiles):
    for a in tiles:
        if a >> bit & 1:
            continue
        b = a + (1 << bit)
        al, ar = halves(load(a))
        bl, br = halves(load(b))
        weights = jnp.concatenate([al, bl, ar, br], axis=0)
        for_a = jnp.concatenate([near[chosen(a, 0)], near[chosen(a, 1)]], axis=1)
        for_b = jnp.concatenate([swapped[chosen(b, 0)], swapped[chosen(b, 1)]], axis=1)
        out = dot(jnp.concatenate([for_a, for_b], axis=0), weights)
        store(a, out[:RANK])
        store(b, out[RANK:])


def lane_level(load, store, near, chosen, tiles):
    for a in tiles:
        tile = load(a)
        al, ar = halves(tile)
        bl, br = halves(swap_halves(tile))
        weights = jnp.concatenate([al, bl, ar, br], axis=0)
        store(a, dot(jnp.concatenate([near[chosen(a, 0)], near[chosen(a, 1)]], axis=1), weights))


def other_level(load, load_partner, store, near, chosen, tiles):
    for a in tiles:
        al, ar = halves(load(a))
        bl, br = halves(load_partner(a))
        weights = jnp.concatenate([al, bl, ar, br], axis=0)
        store(a, dot(jnp.concatenate([near[chosen(a, 0)], near[chosen(a, 1)]], axis=1), weights))


def getter(ref):
    return lambda tile: ref[tile]


def setter(ref):
    def store(tile, value):
        ref[tile] = value

    return store


def col_place():
    return lax.axis_index("yh") * 4 + lax.axis_index("x")


def row_low():
    return lax.axis_index("yl") * 4 + lax.axis_index("z")


def leaf_kernel(maps, vectors, out, v_in, x_in, made, v_sem, x_sem, out_sem):
    copies = []
    for n in range(2):
        rows = pl.ds(n * 64, 64)
        copies.append(
            (
                pltpu.make_async_copy(maps.at[rows], v_in.at[rows], v_sem.at[n]),
                pltpu.make_async_copy(vectors.at[rows], x_in.at[rows], x_sem.at[n]),
            )
        )
        for copy in copies[-1]:
            copy.start()
    zero = jnp.zeros((LEAF // 2, WIDE), jnp.bfloat16)
    sent = []
    for h in range(8):
        if h % 4 == 0:
            for copy in copies[h // 4]:
                copy.wait()
        rows = pl.ds(h * 16, 16)
        maps_here = v_in[rows].reshape(16, LEAF // 2, WIDE)
        vectors_here = x_in[rows].reshape(16, LEAF // 2, WIDE)
        for tile in range(0, 8, 2):
            order = [tile + step for step in (0, 8, 1, 9)]
            v = jnp.concatenate([maps_here[j] for j in order], axis=0).T
            lhs = jnp.concatenate([v[:RANK], v[RANK:]], axis=1)
            even, odd = [], []
            for place, j in enumerate(order):
                raw = vectors_here[j]
                el, orr = halves(raw)
                ol, er = halves(swap_halves(raw))
                e, o = (el, ol) if place % 2 == 0 else (er, orr)
                even.append([e, zero] if place < 2 else [zero, e])
                odd.append([o, zero] if place < 2 else [zero, o])
            weights = jnp.concatenate([jnp.concatenate(r, axis=1) for r in even + odd], axis=0)
            both = dot(lhs, weights)
            made[h * 8 + tile] = both[:, :WIDE]
            made[h * 8 + tile + 1] = both[:, WIDE:]
        if h % 4 == 3:
            done = pl.ds((h - 3) * 8, 32)
            sent.append(pltpu.make_async_copy(made.at[done], out.at[done], out_sem.at[h // 4]))
            sent[-1].start()
    for copy in sent:
        copy.wait()


def table_kernel(
    patterns, late_patterns, translations, first_chosen, second_chosen, near, swapped, p_in, p_sem, t_sem
):
    table = pltpu.make_async_copy(translations, near, t_sem)
    table.start()
    core = lax.axis_index("core")
    lookups = []
    for k in range(8):
        columns = pl.ds(pl.multiple_of((k * 16 + row_low() * 2 + core) * 128, 128), 128)
        lookups.append(pltpu.make_async_copy(patterns.at[pl.ds(0, 8), columns], p_in.at[k], p_sem.at[k]))
        lookups[k].start()
    lane = lax.broadcasted_iota(jnp.int32, (8, 128), 1)
    first = second = jnp.zeros((8, 128), jnp.int32)
    for k in range(8):
        turn = jnp.remainder(k - row_low() + 128, 128)
        rows = late_patterns[:, pl.ds(pl.multiple_of((k * 2 + core) * 128, 128), 128)]
        second = jnp.where((lane & 7) == k, pltpu.roll(rows, turn, 1), second)
    second_chosen[...] = second
    for k in range(8):
        lookups[k].wait()
    for k in range(8):
        turn = jnp.remainder((k - col_place()) * 16 + 128, 128)
        first = jnp.where((lane >> 4) == k, pltpu.roll(p_in[k], turn, 1), first)
    first_chosen[...] = first
    table.wait()
    for m in range(near.shape[0]):
        swapped[m] = swap_halves(near[m])


def chip_order(tile):
    col, row = tile >> 3, tile & 7
    return (col & 3) * 16 + (row & 3) * 4 + (col >> 2) * 2 + (row >> 2)


def lane_of(tile, half):
    return (tile >> 3) * 16 + half * 8 + (tile & 7)


def lookup(chosen_ref, level):
    row = chosen_ref[level : level + 1, :]
    return lambda tile, half: row[0, lane_of(tile, half)]


def first_kernel(chosen_ref, state, near, swapped, out, one, two, spread):
    for level in range(7):
        spread[level] = jnp.broadcast_to(chosen_ref[level : level + 1, :], (128, 128)).T

    def lookup(level):
        return lambda tile, half: spread[level, lane_of(tile, half) : lane_of(tile, half) + 1, :][0, 0]

    every = range(TILES)
    bufs = [state, one, two, one, two, one, two]
    for level, bit in enumerate((3, 4, 5, 0, 1, 2)):
        tile_level(
            getter(bufs[level]), setter(bufs[level + 1]), near, swapped, lookup(level), bit, every
        )

    def store(tile, value):
        out[chip_order(tile)] = value

    lane_level(getter(two), store, near, lookup(6), every)


HALVES = [[tile for tile in range(TILES) if tile >> 2 & 1 == n] for n in range(2)]


def packed(tile):
    return (tile >> 3) * 4 + (tile & 3)


def second_kernel(part, chosen_ref, state, near, swapped, out, one, two):
    tiles = HALVES[part]

    def store_out(tile, value):
        out[packed(tile)] = value

    loads = [lambda tile: state[chip_order(tile)], getter(one), getter(two)]
    stores = [setter(one), setter(two), store_out]
    for level in range(3):
        tile_level(
            loads[level], stores[level], near, swapped, lookup(chosen_ref, 1 + level), 3 + level, tiles
        )


def row_levels(part, chosen_ref, state, partner, near, swapped, one, two, store):
    tiles = HALVES[part]
    load, load_partner = (lambda tile, ref=ref: ref[packed(tile)] for ref in (state, partner))
    other_level(load, load_partner, setter(one), near, lookup(chosen_ref, 4), tiles)
    tile_level(getter(one), setter(two), near, swapped, lookup(chosen_ref, 5), 0, tiles)
    tile_level(getter(two), store, near, swapped, lookup(chosen_ref, 6), 1, tiles)


def third_kernel(chosen_ref, state, partner, near, swapped, out, one, two):
    def store(tile, value):
        out[packed(tile)] = value

    row_levels(0, chosen_ref, state, partner, near, swapped, one, two, store)


def fourth_kernel(chosen_ref, earlier, state, partner, near, swapped, out, one, two):
    row_levels(1, chosen_ref, state, partner, near, swapped, one, two, setter(one))
    load = lambda tile: one[tile] if tile >> 2 & 1 else earlier[packed(tile)]

    def store(tile, value):
        out[(tile & 7) * 8 + (tile >> 3)] = value

    tile_level(load, store, near, swapped, lookup(chosen_ref, 7), 2, range(TILES))


def expand_kernel(state, maps, out, made, sem):
    copies = []
    zero = jnp.zeros((LEAF // 2, WIDE), jnp.bfloat16)
    for h in range(8):
        rows = pl.ds(h * 16, 16)
        maps_here = maps[rows].reshape(16, LEAF // 2, WIDE)
        results = [None] * 16
        for q in range(8):
            both = state[q * 8 + h]
            al, ar = halves(both)
            bl, br = halves(swap_halves(both))
            lhs = [[maps_here[q], zero], [zero, maps_here[q + 8]]]
            lhs = jnp.concatenate([jnp.concatenate(r, axis=1) for r in lhs], axis=0)
            two = dot(lhs, jnp.concatenate([al, br, bl, ar], axis=0))
            results[q], results[q + 8] = two[: LEAF // 2], two[LEAF // 2 :]
        made[rows] = jnp.stack(results, axis=0).reshape(16, LEAF * VECS)
        copies.append(pltpu.make_async_copy(made.at[rows], out.at[rows], sem.at[h]))
        copies[-1].start()
    for copy in copies:
        copy.wait()


VM = pl.BlockSpec(memory_space=pltpu.VMEM)
HB = pl.BlockSpec(memory_space=pltpu.HBM)
PARAMS = pltpu.CompilerParams(vmem_limit_bytes=32 * 1024 * 1024)
STATE = jax.ShapeDtypeStruct((TILES, RANK, WIDE), jnp.bfloat16)
HALF = jax.ShapeDtypeStruct((TILES // 2, RANK, WIDE), jnp.bfloat16)


def make_tables(patterns, translations):
    late_patterns = lax.dynamic_slice(patterns, (6, col_place() * 2048), (8, 2048))
    table = jax.ShapeDtypeStruct(translations.shape, translations.dtype)
    return pl.pallas_call(
        table_kernel,
        out_shape=[
            jax.ShapeDtypeStruct((8, 128), jnp.int32), jax.ShapeDtypeStruct((8, 128), jnp.int32), table, table,
        ],
        in_specs=[HB, VM, HB], out_specs=[VM] * 4,
        scratch_shapes=[
            pltpu.VMEM((8, 8, 128), jnp.int32), pltpu.SemaphoreType.DMA((8,)), pltpu.SemaphoreType.DMA,
        ],
        compiler_params=PARAMS,
    )(patterns, late_patterns, translations)


def local(inputs, leaf_maps, expand_maps, patterns, translations):
    rows = jax.ShapeDtypeStruct(inputs.shape, jnp.bfloat16)
    scratch = [pltpu.VMEM(STATE.shape, STATE.dtype)] * 2
    state = pl.pallas_call(
        leaf_kernel, out_shape=STATE, in_specs=[HB] * 2, out_specs=HB,
        scratch_shapes=[pltpu.VMEM(rows.shape, rows.dtype)] * 2
        + [pltpu.VMEM(STATE.shape, STATE.dtype)] + [pltpu.SemaphoreType.DMA((2,))] * 3,
        compiler_params=pltpu.CompilerParams(vmem_limit_bytes=63 * 1024 * 1024),
    )(leaf_maps, inputs)
    first_chosen, second_chosen, near, swapped = make_tables(patterns, translations)
    state = lax.all_to_all(state, ("yh", "x"), 0, 0, tiled=True)
    state = pl.pallas_call(
        first_kernel, out_shape=STATE, in_specs=[VM, VM, VM, VM], out_specs=VM,
        scratch_shapes=scratch + [pltpu.VMEM((7, 128, 128), jnp.int32)], compiler_params=PARAMS,
    )(first_chosen, state, near, swapped)
    state = lax.all_to_all(state, CHIPS, 0, 0, tiled=True)
    parts, partners = [], []
    for n in range(2):
        parts.append(
            pl.pallas_call(
                functools.partial(second_kernel, n), out_shape=HALF, in_specs=[VM, VM, VM, VM], out_specs=VM,
                scratch_shapes=scratch, compiler_params=PARAMS,
            )(second_chosen, state, near, swapped)
        )
        partners.append(lax.ppermute(parts[n], "core", [(0, 1), (1, 0)]))
    earlier = pl.pallas_call(
        third_kernel, out_shape=HALF, in_specs=[VM, VM, VM, VM, VM], out_specs=VM,
        scratch_shapes=scratch, compiler_params=PARAMS,
    )(second_chosen, parts[0], partners[0], near, swapped)
    state = pl.pallas_call(
        fourth_kernel, out_shape=STATE, in_specs=[VM, VM, VM, VM, VM, VM], out_specs=VM,
        scratch_shapes=scratch, compiler_params=PARAMS,
    )(second_chosen, earlier, parts[1], partners[1], near, swapped)
    state = lax.all_to_all(state, ("yl", "z"), 0, 0, tiled=True)
    return pl.pallas_call(
        expand_kernel, out_shape=rows, in_specs=[VM, VM], out_specs=HB,
        scratch_shapes=[pltpu.VMEM(rows.shape, rows.dtype), pltpu.SemaphoreType.DMA((8,))],
        compiler_params=PARAMS,
    )(state, expand_maps)


def solution(mesh):
    fine = Mesh(mesh.devices.reshape(2, 4, 2, 4, 2), AXES)
    rows = P(AXES, None)
    return jax.shard_map(
        local, mesh=fine, in_specs=(rows, rows, rows, P(), P()), out_specs=rows, check_vma=False
    )
```

```python
import functools

import jax
import jax.numpy as jnp
from jax import lax
from jax.experimental import pallas as pl
from jax.experimental.pallas import tpu as pltpu
from jax.sharding import Mesh, PartitionSpec as P

LEAF = 64
RANK = 64
VECS = 64
WIDE = 2 * VECS
TILES = 64
AXES = ("yh", "x", "yl", "z", "core")
CHIPS = ("z", "x", "yh", "yl")


def left_half(shape):
    return lax.broadcasted_iota(jnp.int32, shape, len(shape) - 1) < VECS


def halves(tile):
    left = left_half(tile.shape)
    zero = jnp.zeros_like(tile)
    return jnp.where(left, tile, zero), jnp.where(left, zero, tile)


def swap_halves(tile):
    return jnp.concatenate([tile[:, VECS:], tile[:, :VECS]], axis=1)


def dot(lhs, rhs):
    return jnp.dot(lhs, rhs, preferred_element_type=jnp.float32).astype(jnp.bfloat16)


def tile_level(load, store, near, swapped, chosen, bit, tiles):
    for a in tiles:
        if a >> bit & 1:
            continue
        b = a + (1 << bit)
        al, ar = halves(load(a))
        bl, br = halves(load(b))
        weights = jnp.concatenate([al, bl, ar, br], axis=0)
        for_a = jnp.concatenate([near[chosen(a, 0)], near[chosen(a, 1)]], axis=1)
        for_b = jnp.concatenate([swapped[chosen(b, 0)], swapped[chosen(b, 1)]], axis=1)
        out = dot(jnp.concatenate([for_a, for_b], axis=0), weights)
        store(a, out[:RANK])
        store(b, out[RANK:])


def lane_level(load, store, near, chosen, tiles):
    for a in tiles:
        tile = load(a)
        al, ar = halves(tile)
        bl, br = halves(swap_halves(tile))
        weights = jnp.concatenate([al, bl, ar, br], axis=0)
        store(a, dot(jnp.concatenate([near[chosen(a, 0)], near[chosen(a, 1)]], axis=1), weights))


def other_level(load, load_partner, store, near, chosen, tiles):
    for a in tiles:
        al, ar = halves(load(a))
        bl, br = halves(load_partner(a))
        weights = jnp.concatenate([al, bl, ar, br], axis=0)
        store(a, dot(jnp.concatenate([near[chosen(a, 0)], near[chosen(a, 1)]], axis=1), weights))


def getter(ref):
    return lambda tile: ref[tile]


def setter(ref):
    def store(tile, value):
        ref[tile] = value

    return store


def col_place():
    return lax.axis_index("yh") * 4 + lax.axis_index("x")


def row_low():
    return lax.axis_index("yl") * 4 + lax.axis_index("z")


def leaf_kernel(maps, vectors, out, v_in, x_in, made, v_sem, x_sem, out_sem):
    copies = []
    for n in range(2):
        rows = pl.ds(n * 64, 64)
        copies.append(
            (
                pltpu.make_async_copy(maps.at[rows], v_in.at[rows], v_sem.at[n]),
                pltpu.make_async_copy(vectors.at[rows], x_in.at[rows], x_sem.at[n]),
            )
        )
        for copy in copies[-1]:
            copy.start()
    zero = jnp.zeros((LEAF // 2, WIDE), jnp.bfloat16)
    sent = []
    for h in range(8):
        if h % 4 == 0:
            for copy in copies[h // 4]:
                copy.wait()
        rows = pl.ds(h * 16, 16)
        maps_here = v_in[rows].reshape(16, LEAF // 2, WIDE)
        vectors_here = x_in[rows].reshape(16, LEAF // 2, WIDE)
        for tile in range(0, 8, 2):
            order = [tile + step for step in (0, 8, 1, 9)]
            v = jnp.concatenate([maps_here[j] for j in order], axis=0).T
            lhs = jnp.concatenate([v[:RANK], v[RANK:]], axis=1)
            even, odd = [], []
            for place, j in enumerate(order):
                raw = vectors_here[j]
                el, orr = halves(raw)
                ol, er = halves(swap_halves(raw))
                e, o = (el, ol) if place % 2 == 0 else (er, orr)
                even.append([e, zero] if place < 2 else [zero, e])
                odd.append([o, zero] if place < 2 else [zero, o])
            weights = jnp.concatenate([jnp.concatenate(r, axis=1) for r in even + odd], axis=0)
            both = dot(lhs, weights)
            made[h * 8 + tile] = both[:, :WIDE]
            made[h * 8 + tile + 1] = both[:, WIDE:]
        if h % 4 == 3:
            done = pl.ds((h - 3) * 8, 32)
            sent.append(pltpu.make_async_copy(made.at[done], out.at[done], out_sem.at[h // 4]))
            sent[-1].start()
    for copy in sent:
        copy.wait()


def table_kernel(
    patterns, late_patterns, translations, first_chosen, second_chosen, near, swapped, p_in, p_sem, t_sem
):
    table = pltpu.make_async_copy(translations, near, t_sem)
    table.start()
    core = lax.axis_index("core")
    lookups = []
    for k in range(8):
        columns = pl.ds(pl.multiple_of((k * 16 + row_low() * 2 + core) * 128, 128), 128)
        lookups.append(pltpu.make_async_copy(patterns.at[pl.ds(0, 8), columns], p_in.at[k], p_sem.at[k]))
        lookups[k].start()
    lane = lax.broadcasted_iota(jnp.int32, (8, 128), 1)
    first = second = jnp.zeros((8, 128), jnp.int32)
    for k in range(8):
        turn = jnp.remainder(k - row_low() + 128, 128)
        rows = late_patterns[:, pl.ds(pl.multiple_of((k * 2 + core) * 128, 128), 128)]
        second = jnp.where((lane & 7) == k, pltpu.roll(rows, turn, 1), second)
    second_chosen[...] = second
    for k in range(8):
        lookups[k].wait()
    for k in range(8):
        turn = jnp.remainder((k - col_place()) * 16 + 128, 128)
        first = jnp.where((lane >> 4) == k, pltpu.roll(p_in[k], turn, 1), first)
    first_chosen[...] = first
    table.wait()
    for m in range(near.shape[0]):
        swapped[m] = swap_halves(near[m])


def chip_order(tile):
    col, row = tile >> 3, tile & 7
    return (row & 3) * 16 + (col & 3) * 4 + (col >> 2) * 2 + (row >> 2)


def lane_of(tile, half):
    return (tile >> 3) * 16 + half * 8 + (tile & 7)


def lookup(chosen_ref, level):
    row = chosen_ref[level : level + 1, :]
    return lambda tile, half: row[0, lane_of(tile, half)]


def first_kernel(chosen_ref, state, near, swapped, out, one, two, spread):
    for level in range(7):
        spread[level] = jnp.broadcast_to(chosen_ref[level : level + 1, :], (128, 128)).T

    def lookup(level):
        return lambda tile, half: spread[level, lane_of(tile, half) : lane_of(tile, half) + 1, :][0, 0]

    every = range(TILES)
    bufs = [state, one, two, one, two, one, two]
    for level, bit in enumerate((3, 4, 5, 0, 1, 2)):
        tile_level(
            getter(bufs[level]), setter(bufs[level + 1]), near, swapped, lookup(level), bit, every
        )

    def store(tile, value):
        out[chip_order(tile)] = value

    lane_level(getter(two), store, near, lookup(6), every)


HALVES = [[tile for tile in range(TILES) if tile >> 2 & 1 == n] for n in range(2)]


def packed(tile):
    return (tile >> 3) * 4 + (tile & 3)


def second_kernel(part, chosen_ref, state, near, swapped, out, one, two):
    tiles = HALVES[part]

    def store_out(tile, value):
        out[packed(tile)] = value

    loads = [lambda tile: state[chip_order(tile)], getter(one), getter(two)]
    stores = [setter(one), setter(two), store_out]
    for level in range(3):
        tile_level(
            loads[level], stores[level], near, swapped, lookup(chosen_ref, 1 + level), 3 + level, tiles
        )


def row_levels(part, chosen_ref, state, partner, near, swapped, one, two, store):
    tiles = HALVES[part]
    load, load_partner = (lambda tile, ref=ref: ref[packed(tile)] for ref in (state, partner))
    other_level(load, load_partner, setter(one), near, lookup(chosen_ref, 4), tiles)
    tile_level(getter(one), setter(two), near, swapped, lookup(chosen_ref, 5), 0, tiles)
    tile_level(getter(two), store, near, swapped, lookup(chosen_ref, 6), 1, tiles)


def third_kernel(chosen_ref, state, partner, near, swapped, out, one, two):
    def store(tile, value):
        out[packed(tile)] = value

    row_levels(0, chosen_ref, state, partner, near, swapped, one, two, store)


def fourth_kernel(chosen_ref, earlier, state, partner, near, swapped, out, one, two):
    row_levels(1, chosen_ref, state, partner, near, swapped, one, two, setter(one))
    load = lambda tile: one[tile] if tile >> 2 & 1 else earlier[packed(tile)]

    def store(tile, value):
        out[(tile & 7) * 8 + (tile >> 3)] = value

    tile_level(load, store, near, swapped, lookup(chosen_ref, 7), 2, range(TILES))


def expand_kernel(state, maps, out, made, sem):
    copies = []
    zero = jnp.zeros((LEAF // 2, WIDE), jnp.bfloat16)
    for h in range(8):
        rows = pl.ds(h * 16, 16)
        maps_here = maps[rows].reshape(16, LEAF // 2, WIDE)
        results = [None] * 16
        for q in range(8):
            both = state[q * 8 + h]
            al, ar = halves(both)
            bl, br = halves(swap_halves(both))
            lhs = [[maps_here[q], zero], [zero, maps_here[q + 8]]]
            lhs = jnp.concatenate([jnp.concatenate(r, axis=1) for r in lhs], axis=0)
            two = dot(lhs, jnp.concatenate([al, br, bl, ar], axis=0))
            results[q], results[q + 8] = two[: LEAF // 2], two[LEAF // 2 :]
        made[rows] = jnp.stack(results, axis=0).reshape(16, LEAF * VECS)
        copies.append(pltpu.make_async_copy(made.at[rows], out.at[rows], sem.at[h]))
        copies[-1].start()
    for copy in copies:
        copy.wait()


VM = pl.BlockSpec(memory_space=pltpu.VMEM)
HB = pl.BlockSpec(memory_space=pltpu.HBM)
PARAMS = pltpu.CompilerParams(vmem_limit_bytes=32 * 1024 * 1024)
STATE = jax.ShapeDtypeStruct((TILES, RANK, WIDE), jnp.bfloat16)
HALF = jax.ShapeDtypeStruct((TILES // 2, RANK, WIDE), jnp.bfloat16)


def make_tables(patterns, translations):
    late_patterns = lax.dynamic_slice(patterns, (6, col_place() * 2048), (8, 2048))
    table = jax.ShapeDtypeStruct(translations.shape, translations.dtype)
    return pl.pallas_call(
        table_kernel,
        out_shape=[
            jax.ShapeDtypeStruct((8, 128), jnp.int32), jax.ShapeDtypeStruct((8, 128), jnp.int32), table, table,
        ],
        in_specs=[HB, VM, HB], out_specs=[VM] * 4,
        scratch_shapes=[
            pltpu.VMEM((8, 8, 128), jnp.int32), pltpu.SemaphoreType.DMA((8,)), pltpu.SemaphoreType.DMA,
        ],
        compiler_params=PARAMS,
    )(patterns, late_patterns, translations)


def local(inputs, leaf_maps, expand_maps, patterns, translations):
    rows = jax.ShapeDtypeStruct(inputs.shape, jnp.bfloat16)
    scratch = [pltpu.VMEM(STATE.shape, STATE.dtype)] * 2
    state = pl.pallas_call(
        leaf_kernel, out_shape=STATE, in_specs=[HB] * 2, out_specs=HB,
        scratch_shapes=[pltpu.VMEM(rows.shape, rows.dtype)] * 2
        + [pltpu.VMEM(STATE.shape, STATE.dtype)] + [pltpu.SemaphoreType.DMA((2,))] * 3,
        compiler_params=pltpu.CompilerParams(vmem_limit_bytes=63 * 1024 * 1024),
    )(leaf_maps, inputs)
    first_chosen, second_chosen, near, swapped = make_tables(patterns, translations)
    state = lax.all_to_all(state, ("yh", "x"), 0, 0, tiled=True)
    state = pl.pallas_call(
        first_kernel, out_shape=STATE, in_specs=[VM, VM, VM, VM], out_specs=VM,
        scratch_shapes=scratch + [pltpu.VMEM((7, 128, 128), jnp.int32)], compiler_params=PARAMS,
    )(first_chosen, state, near, swapped)
    state = lax.all_to_all(state, CHIPS, 0, 0, tiled=True)
    parts, partners = [], []
    for n in range(2):
        parts.append(
            pl.pallas_call(
                functools.partial(second_kernel, n), out_shape=HALF, in_specs=[VM, VM, VM, VM], out_specs=VM,
                scratch_shapes=scratch, compiler_params=PARAMS,
            )(second_chosen, state, near, swapped)
        )
        partners.append(lax.ppermute(parts[n], "core", [(0, 1), (1, 0)]))
    earlier = pl.pallas_call(
        third_kernel, out_shape=HALF, in_specs=[VM, VM, VM, VM, VM], out_specs=VM,
        scratch_shapes=scratch, compiler_params=PARAMS,
    )(second_chosen, parts[0], partners[0], near, swapped)
    state = pl.pallas_call(
        fourth_kernel, out_shape=STATE, in_specs=[VM, VM, VM, VM, VM, VM], out_specs=VM,
        scratch_shapes=scratch, compiler_params=PARAMS,
    )(second_chosen, earlier, parts[1], partners[1], near, swapped)
    state = lax.all_to_all(state, ("yl", "z"), 0, 0, tiled=True)
    return pl.pallas_call(
        expand_kernel, out_shape=rows, in_specs=[VM, VM], out_specs=HB,
        scratch_shapes=[pltpu.VMEM(rows.shape, rows.dtype), pltpu.SemaphoreType.DMA((8,))],
        compiler_params=PARAMS,
    )(state, expand_maps)


def solution(mesh):
    fine = Mesh(mesh.devices.reshape(2, 4, 2, 4, 2), AXES)
    rows = P(AXES, None)
    return jax.shard_map(
        local, mesh=fine, in_specs=(rows, rows, rows, P(), P()), out_specs=rows, check_vma=False
    )
```

```python
import functools

import jax
import jax.numpy as jnp
from jax import lax
from jax.experimental import pallas as pl
from jax.experimental.pallas import tpu as pltpu
from jax.sharding import Mesh, PartitionSpec as P

LEAF = 64
RANK = 64
VECS = 64
WIDE = 2 * VECS
TILES = 64
AXES = ("yh", "x", "yl", "z", "core")
CHIPS = ("x", "z", "yh", "yl")


def left_half(shape):
    return lax.broadcasted_iota(jnp.int32, shape, len(shape) - 1) < VECS


def halves(tile):
    left = left_half(tile.shape)
    zero = jnp.zeros_like(tile)
    return jnp.where(left, tile, zero), jnp.where(left, zero, tile)


def swap_halves(tile):
    return jnp.concatenate([tile[:, VECS:], tile[:, :VECS]], axis=1)


def dot(lhs, rhs):
    return jnp.dot(lhs, rhs, preferred_element_type=jnp.float32).astype(jnp.bfloat16)


def tile_level(load, store, near, swapped, chosen, bit, tiles):
    for a in tiles:
        if a >> bit & 1:
            continue
        b = a + (1 << bit)
        al, ar = halves(load(a))
        bl, br = halves(load(b))
        weights = jnp.concatenate([al, bl, ar, br], axis=0)
        for_a = jnp.concatenate([near[chosen(a, 0)], near[chosen(a, 1)]], axis=1)
        for_b = jnp.concatenate([swapped[chosen(b, 0)], swapped[chosen(b, 1)]], axis=1)
        out = dot(jnp.concatenate([for_a, for_b], axis=0), weights)
        store(a, out[:RANK])
        store(b, out[RANK:])


def lane_level(load, store, near, chosen, tiles):
    for a in tiles:
        tile = load(a)
        al, ar = halves(tile)
        bl, br = halves(swap_halves(tile))
        weights = jnp.concatenate([al, bl, ar, br], axis=0)
        store(a, dot(jnp.concatenate([near[chosen(a, 0)], near[chosen(a, 1)]], axis=1), weights))


def other_level(load, load_partner, store, near, chosen, tiles):
    for a in tiles:
        al, ar = halves(load(a))
        bl, br = halves(load_partner(a))
        weights = jnp.concatenate([al, bl, ar, br], axis=0)
        store(a, dot(jnp.concatenate([near[chosen(a, 0)], near[chosen(a, 1)]], axis=1), weights))


def getter(ref):
    return lambda tile: ref[tile]


def setter(ref):
    def store(tile, value):
        ref[tile] = value

    return store


def col_place():
    return lax.axis_index("yh") * 4 + lax.axis_index("x")


def row_low():
    return lax.axis_index("yl") * 4 + lax.axis_index("z")


def leaf_kernel(maps, vectors, out, v_in, x_in, made, v_sem, x_sem, out_sem):
    copies = []
    for n in range(2):
        rows = pl.ds(n * 64, 64)
        copies.append(
            (
                pltpu.make_async_copy(maps.at[rows], v_in.at[rows], v_sem.at[n]),
                pltpu.make_async_copy(vectors.at[rows], x_in.at[rows], x_sem.at[n]),
            )
        )
        for copy in copies[-1]:
            copy.start()
    zero = jnp.zeros((LEAF // 2, WIDE), jnp.bfloat16)
    sent = []
    for h in range(8):
        if h % 4 == 0:
            for copy in copies[h // 4]:
                copy.wait()
        rows = pl.ds(h * 16, 16)
        maps_here = v_in[rows].reshape(16, LEAF // 2, WIDE)
        vectors_here = x_in[rows].reshape(16, LEAF // 2, WIDE)
        for tile in range(0, 8, 2):
            order = [tile + step for step in (0, 8, 1, 9)]
            v = jnp.concatenate([maps_here[j] for j in order], axis=0).T
            lhs = jnp.concatenate([v[:RANK], v[RANK:]], axis=1)
            even, odd = [], []
            for place, j in enumerate(order):
                raw = vectors_here[j]
                el, orr = halves(raw)
                ol, er = halves(swap_halves(raw))
                e, o = (el, ol) if place % 2 == 0 else (er, orr)
                even.append([e, zero] if place < 2 else [zero, e])
                odd.append([o, zero] if place < 2 else [zero, o])
            weights = jnp.concatenate([jnp.concatenate(r, axis=1) for r in even + odd], axis=0)
            both = dot(lhs, weights)
            made[h * 8 + tile] = both[:, :WIDE]
            made[h * 8 + tile + 1] = both[:, WIDE:]
        if h % 4 == 3:
            done = pl.ds((h - 3) * 8, 32)
            sent.append(pltpu.make_async_copy(made.at[done], out.at[done], out_sem.at[h // 4]))
            sent[-1].start()
    for copy in sent:
        copy.wait()


def table_kernel(
    patterns, late_patterns, translations, first_chosen, second_chosen, near, swapped, p_in, p_sem, t_sem
):
    table = pltpu.make_async_copy(translations, near, t_sem)
    table.start()
    core = lax.axis_index("core")
    lookups = []
    for k in range(8):
        columns = pl.ds(pl.multiple_of((k * 16 + row_low() * 2 + core) * 128, 128), 128)
        lookups.append(pltpu.make_async_copy(patterns.at[pl.ds(0, 8), columns], p_in.at[k], p_sem.at[k]))
        lookups[k].start()
    lane = lax.broadcasted_iota(jnp.int32, (8, 128), 1)
    first = second = jnp.zeros((8, 128), jnp.int32)
    for k in range(8):
        turn = jnp.remainder(k - row_low() + 128, 128)
        rows = late_patterns[:, pl.ds(pl.multiple_of((k * 2 + core) * 128, 128), 128)]
        second = jnp.where((lane & 7) == k, pltpu.roll(rows, turn, 1), second)
    second_chosen[...] = second
    for k in range(8):
        lookups[k].wait()
    for k in range(8):
        turn = jnp.remainder((k - col_place()) * 16 + 128, 128)
        first = jnp.where((lane >> 4) == k, pltpu.roll(p_in[k], turn, 1), first)
    first_chosen[...] = first
    table.wait()
    for m in range(near.shape[0]):
        swapped[m] = swap_halves(near[m])


def chip_order(tile):
    col, row = tile >> 3, tile & 7
    return (col & 3) * 16 + (row & 3) * 4 + (col >> 2) * 2 + (row >> 2)


def lane_of(tile, half):
    return (tile >> 3) * 16 + half * 8 + (tile & 7)


def lookup(chosen_ref, level):
    row = chosen_ref[level : level + 1, :]
    return lambda tile, half: row[0, lane_of(tile, half)]


def first_kernel(chosen_ref, state, near, swapped, out, one, two):
    every = range(TILES)
    bufs = [state, one, two, one, two, one, two]
    for level, bit in enumerate((3, 4, 5, 0, 1, 2)):
        tile_level(
            getter(bufs[level]), setter(bufs[level + 1]), near, swapped, lookup(chosen_ref, level), bit, every
        )

    def store(tile, value):
        out[chip_order(tile)] = value

    lane_level(getter(two), store, near, lookup(chosen_ref, 6), every)


HALVES = [[tile for tile in range(TILES) if tile >> 2 & 1 == n] for n in range(2)]


def packed(tile):
    return (tile >> 3) * 4 + (tile & 3)


def second_kernel(part, chosen_ref, state, near, swapped, out, one, two):
    tiles = HALVES[part]

    def store_out(tile, value):
        out[packed(tile)] = value

    loads = [lambda tile: state[chip_order(tile)], getter(one), getter(two)]
    stores = [setter(one), setter(two), store_out]
    for level in range(3):
        tile_level(
            loads[level], stores[level], near, swapped, lookup(chosen_ref, 1 + level), 3 + level, tiles
        )


def row_levels(part, chosen_ref, state, partner, near, swapped, one, two, store):
    tiles = HALVES[part]
    load, load_partner = (lambda tile, ref=ref: ref[packed(tile)] for ref in (state, partner))
    other_level(load, load_partner, setter(one), near, lookup(chosen_ref, 4), tiles)
    tile_level(getter(one), setter(two), near, swapped, lookup(chosen_ref, 5), 0, tiles)
    tile_level(getter(two), store, near, swapped, lookup(chosen_ref, 6), 1, tiles)


def third_kernel(chosen_ref, state, partner, near, swapped, out, one, two):
    def store(tile, value):
        out[packed(tile)] = value

    row_levels(0, chosen_ref, state, partner, near, swapped, one, two, store)


def fourth_kernel(chosen_ref, earlier, state, partner, near, swapped, out, one, two):
    row_levels(1, chosen_ref, state, partner, near, swapped, one, two, setter(one))
    load = lambda tile: one[tile] if tile >> 2 & 1 else earlier[packed(tile)]

    def store(tile, value):
        out[(tile & 7) * 8 + (tile >> 3)] = value

    tile_level(load, store, near, swapped, lookup(chosen_ref, 7), 2, range(TILES))


def expand_kernel(state, maps, out, made, sem):
    copies = []
    zero = jnp.zeros((LEAF // 2, WIDE), jnp.bfloat16)
    for h in range(8):
        rows = pl.ds(h * 16, 16)
        maps_here = maps[rows].reshape(16, LEAF // 2, WIDE)
        results = [None] * 16
        for q in range(8):
            both = state[q * 8 + h]
            al, ar = halves(both)
            bl, br = halves(swap_halves(both))
            lhs = [[maps_here[q], zero], [zero, maps_here[q + 8]]]
            lhs = jnp.concatenate([jnp.concatenate(r, axis=1) for r in lhs], axis=0)
            two = dot(lhs, jnp.concatenate([al, br, bl, ar], axis=0))
            results[q], results[q + 8] = two[: LEAF // 2], two[LEAF // 2 :]
        made[rows] = jnp.stack(results, axis=0).reshape(16, LEAF * VECS)
        copies.append(pltpu.make_async_copy(made.at[rows], out.at[rows], sem.at[h]))
        copies[-1].start()
    for copy in copies:
        copy.wait()


VM = pl.BlockSpec(memory_space=pltpu.VMEM)
HB = pl.BlockSpec(memory_space=pltpu.HBM)
PARAMS = pltpu.CompilerParams(vmem_limit_bytes=32 * 1024 * 1024)
STATE = jax.ShapeDtypeStruct((TILES, RANK, WIDE), jnp.bfloat16)
HALF = jax.ShapeDtypeStruct((TILES // 2, RANK, WIDE), jnp.bfloat16)


def make_tables(patterns, translations):
    late_patterns = lax.dynamic_slice(patterns, (6, col_place() * 2048), (8, 2048))
    table = jax.ShapeDtypeStruct(translations.shape, translations.dtype)
    return pl.pallas_call(
        table_kernel,
        out_shape=[
            jax.ShapeDtypeStruct((8, 128), jnp.int32), jax.ShapeDtypeStruct((8, 128), jnp.int32), table, table,
        ],
        in_specs=[HB, VM, HB], out_specs=[VM] * 4,
        scratch_shapes=[
            pltpu.VMEM((8, 8, 128), jnp.int32), pltpu.SemaphoreType.DMA((8,)), pltpu.SemaphoreType.DMA,
        ],
        compiler_params=PARAMS,
    )(patterns, late_patterns, translations)


def local(inputs, leaf_maps, expand_maps, patterns, translations):
    rows = jax.ShapeDtypeStruct(inputs.shape, jnp.bfloat16)
    scratch = [pltpu.VMEM(STATE.shape, STATE.dtype)] * 2
    state = pl.pallas_call(
        leaf_kernel, out_shape=STATE, in_specs=[HB] * 2, out_specs=HB,
        scratch_shapes=[pltpu.VMEM(rows.shape, rows.dtype)] * 2
        + [pltpu.VMEM(STATE.shape, STATE.dtype)] + [pltpu.SemaphoreType.DMA((2,))] * 3,
        compiler_params=pltpu.CompilerParams(vmem_limit_bytes=63 * 1024 * 1024),
    )(leaf_maps, inputs)
    first_chosen, second_chosen, near, swapped = make_tables(patterns, translations)
    state = lax.all_to_all(state, ("yh", "x"), 0, 0, tiled=True)
    state = pl.pallas_call(
        first_kernel, out_shape=STATE, in_specs=[VM, VM, VM, VM], out_specs=VM,
        scratch_shapes=scratch, compiler_params=PARAMS,
    )(first_chosen, state, near, swapped)
    state = lax.all_to_all(state, CHIPS, 0, 0, tiled=True)
    parts, partners = [], []
    for n in range(2):
        parts.append(
            pl.pallas_call(
                functools.partial(second_kernel, n), out_shape=HALF, in_specs=[VM, VM, VM, VM], out_specs=VM,
                scratch_shapes=scratch, compiler_params=PARAMS,
            )(second_chosen, state, near, swapped)
        )
        partners.append(lax.ppermute(parts[n], "core", [(0, 1), (1, 0)]))
    earlier = pl.pallas_call(
        third_kernel, out_shape=HALF, in_specs=[VM, VM, VM, VM, VM], out_specs=VM,
        scratch_shapes=scratch, compiler_params=PARAMS,
    )(second_chosen, parts[0], partners[0], near, swapped)
    state = pl.pallas_call(
        fourth_kernel, out_shape=STATE, in_specs=[VM, VM, VM, VM, VM, VM], out_specs=VM,
        scratch_shapes=scratch, compiler_params=PARAMS,
    )(second_chosen, earlier, parts[1], partners[1], near, swapped)
    state = lax.all_to_all(state, ("yl", "z"), 0, 0, tiled=True)
    return pl.pallas_call(
        expand_kernel, out_shape=rows, in_specs=[VM, VM], out_specs=HB,
        scratch_shapes=[pltpu.VMEM(rows.shape, rows.dtype), pltpu.SemaphoreType.DMA((8,))],
        compiler_params=PARAMS,
    )(state, expand_maps)


def solution(mesh):
    fine = Mesh(mesh.devices.reshape(2, 4, 2, 4, 2), AXES)
    rows = P(AXES, None)
    return jax.shard_map(
        local, mesh=fine, in_specs=(rows, rows, rows, P(), P()), out_specs=rows, check_vma=False
    )
```
